128 devices in a mesh: group: 16 (over z, y), local: 8 (over x, core).
Axes of the slice: x: 4, y: 4, z: 4, core: 2. Of those that a mesh axis runs over, the one named last changes fastest.
Arguments:
- hidden: float32 [2, 128, 7168], P(None, ('group', 'local')), may hold values from -6 to 6
- routes: int32 [2, 128, 8], P(None, ('group', 'local')), may hold values from 0 to 31, as said below
- slots: int32 [2, 128, 8], P(None, ('group', 'local')), may hold values from -1 to 95, as said below
- route_weight: bfloat16 [2, 128, 8], P(None, ('group', 'local')), may hold values from 0.049804688 to 0.5
- expert_gate: bfloat16 [32, 7168, 2048], P('group', None, 'local'), may hold values from -0.0625 to 0.0625
- expert_up: bfloat16 [32, 7168, 2048], P('group', None, 'local'), may hold values from -0.0625 to 0.0625
- expert_down: bfloat16 [32, 2048, 7168], P('group', 'local'), may hold values from -0.125 to 0.125
- shared_gate: bfloat16 [7168, 2048], P(None, ('group', 'local')), may hold values from -0.0625 to 0.0625
- shared_up: bfloat16 [7168, 2048], P(None, ('group', 'local')), may hold values from -0.0625 to 0.0625
- shared_down: bfloat16 [2048, 7168], P(('group', 'local')), may hold values from -0.125 to 0.125
Outputs:
- moe_output: float32 [2, 128, 7168], P(None, ('group', 'local'))
The draws below stay inside these ranges and needn't reach their ends.
Inputs may be any that keep to these rules, and one draw needn't show every extreme that they name: `routes`: each row names 8 different experts, all within at most 4 node groups, node group n holding experts 4 n to 4 n + 3. `slots`: the slot of a route is the number of earlier routes of the same step to the same expert (rows in order, then the routes of a row in order) if that number is under 96, else -1; in every step some expert is named by more than 96 routes.
All inputs are finite; a program needn't handle non-finite values.
Results may differ from the reference program's by a relative error of at most 0.005.
Values may be sent and summed in bfloat16 or wider, within the bound.
No kernel may reach another device: no remote copies, remote signals or barrier semaphores. Data moves between devices by JAX's collectives and lax.ppermute only.
A program may use at most 128 MiB of HBM per device.

```python
import math
import jax
import jax.numpy as jnp
from jax import lax

D = 7168
EXP_FF = 2048
SHARED_FF = 2048
TOP = 8
STEPS = 2
TOKENS = 128
EXPERTS = 32
CAP = 96


def route_table(key):
    keys = jax.random.split(key, 6)
    nodes = EXPERTS // 4
    node_ids = jnp.arange(nodes, dtype=jnp.int32)
    expert_ids = jnp.arange(EXPERTS, dtype=jnp.int32)
    hot_node = jax.random.randint(keys[0], (), 0, nodes)
    node_bias = jax.random.randint(keys[1], (nodes,), 0, 400) + 800 * (node_ids == hot_node).astype(jnp.int32)
    hot_expert = 4 * hot_node + jax.random.randint(keys[2], (), 0, 4)
    expert_bias = jax.random.randint(keys[3], (EXPERTS,), 0, 400) + 800 * (expert_ids == hot_expert).astype(jnp.int32)
    node_score = (jax.random.randint(keys[4], (STEPS, TOKENS, nodes), 0, 1000) + node_bias) * nodes + node_ids
    unused_a, chosen = lax.top_k(node_score, 4)
    candidates = (chosen[..., :, None] * 4 + jnp.arange(4, dtype=jnp.int32)).reshape(STEPS, TOKENS, 16).astype(jnp.int32)
    expert_score = (jax.random.randint(keys[5], (STEPS, TOKENS, 16), 0, 1000) + expert_bias[candidates]) * EXPERTS + candidates
    unused_b, picked = lax.top_k(expert_score, TOP)
    routes = jnp.take_along_axis(candidates, picked, axis=-1).astype(jnp.int32)
    onehot = (routes.reshape(STEPS, TOKENS * TOP)[..., None] == expert_ids).astype(jnp.int32)
    position = jnp.sum((jnp.cumsum(onehot, axis=1) - 1) * onehot, axis=-1)
    slots = jnp.where(position < CAP, position, -1).reshape(STEPS, TOKENS, TOP).astype(jnp.int32)
    return (routes, slots)


def draw_routes(key, part):
    table = route_table(key)
    return table[0]


def draw_slots(key, part):
    table = route_table(key)
    return table[1]


def block_scale(stream_key, shape, cuts, smallest, high):
    level, own = 1.0, jax.random.fold_in(stream_key, 6)
    for dim, parts in cuts:
        steps = jnp.exp(jax.random.uniform(jax.random.fold_in(own, dim), (parts,), jnp.float32, smallest / len(cuts), high / len(cuts)))
        level = level * jnp.repeat(steps, shape[dim] // parts).reshape([-1 if axis == dim else 1 for axis in range(len(shape))])
    return level


def normal_values(own_key, extent, width, reach, cuts=(), held_as=jnp.bfloat16):
    level = block_scale(own_key, extent, cuts, -0.22, 0.18) if cuts else 1.0
    values = jax.random.normal(own_key, extent, jnp.float32) * width * level
    return jnp.minimum(jnp.maximum(values, -reach), reach).astype(held_as)


def setup_inputs(seed: int = 0) -> dict:
    key_of = jax.random.split(jax.random.key(seed), 11)
    hidden = normal_values(key_of[0], (STEPS, TOKENS, D), 1.0, 6.0, ((1, 128),), jnp.float32)
    routes = draw_routes(jax.random.fold_in(key_of[10], 71), 0)
    slots = draw_slots(jax.random.fold_in(key_of[10], 71), 0)
    route_weight = jnp.clip(jnp.exp(math.log(0.5) - 2.306499 * jax.random.uniform(key_of[3], (STEPS, TOKENS, TOP), jnp.float32) ** block_scale(key_of[3], (STEPS, TOKENS, TOP), ((1, 128),), -0.2, 0.2)), 0.049804688, 0.5).astype(jnp.bfloat16)
    expert_gate = normal_values(key_of[4], (EXPERTS, D, EXP_FF), D ** -0.5, 0.0625, ((0, 16), (2, 8)))
    expert_up = normal_values(key_of[5], (EXPERTS, D, EXP_FF), D ** -0.5, 0.0625, ((0, 16), (2, 8)))
    expert_down = normal_values(key_of[6], (EXPERTS, EXP_FF, D), EXP_FF ** -0.5, 0.125, ((0, 16), (1, 8)))
    shared_gate = normal_values(key_of[7], (D, SHARED_FF), D ** -0.5, 0.0625, ((1, 128),))
    shared_up = normal_values(key_of[8], (D, SHARED_FF), D ** -0.5, 0.0625, ((1, 128),))
    shared_down = normal_values(key_of[9], (SHARED_FF, D), SHARED_FF ** -0.5, 0.125, ((0, 128),))
    return dict(hidden=hidden, routes=routes, slots=slots, route_weight=route_weight, expert_gate=expert_gate, expert_up=expert_up, expert_down=expert_down, shared_gate=shared_gate, shared_up=shared_up, shared_down=shared_down)


def expert_block(rows, gate_w, up_w, down_w):
    gate_act = jnp.dot(rows, gate_w, preferred_element_type=jnp.float32)
    up_act = jnp.dot(rows, up_w, preferred_element_type=jnp.float32)
    units = (jax.nn.silu(gate_act) * up_act).astype(jnp.bfloat16)
    return jnp.dot(units, down_w, preferred_element_type=jnp.float32)


def fill_buffer(rounded, routes_flat, slots_flat, expert, capacity, per_row):
    count = routes_flat.shape[0]
    token_ids = (jnp.arange(count, dtype=jnp.int32) // per_row).astype(jnp.int32)
    match = (routes_flat == expert) & (slots_flat >= 0)
    hits = match[:, None] & (slots_flat[:, None] == jnp.arange(capacity, dtype=jnp.int32)[None, :])
    source = jnp.sum(jnp.where(hits, token_ids[:, None], 0), axis=0).astype(jnp.int32)
    present = jnp.any(hits, axis=0)
    return jnp.where(present[:, None], rounded[source], jnp.zeros((), jnp.bfloat16))


def reference(hidden, routes, slots, route_weight, expert_gate, expert_up, expert_down, shared_gate, shared_up, shared_down):
    results = []
    for step in range(STEPS):
        rounded = hidden[step].astype(jnp.bfloat16)
        route_rows = routes[step]
        slot_rows = slots[step]
        weight_rows = route_weight[step].astype(jnp.float32)
        routes_flat = route_rows.reshape(-1)
        slots_flat = slot_rows.reshape(-1)

        def one_expert(expert):
            buffer = fill_buffer(rounded, routes_flat, slots_flat, expert, CAP, TOP)
            return expert_block(buffer, expert_gate[expert], expert_up[expert], expert_down[expert])

        outputs = lax.map(one_expert, jnp.arange(EXPERTS, dtype=jnp.int32)).reshape(EXPERTS * CAP, D)
        total = expert_block(rounded, shared_gate, shared_up, shared_down)
        for route in range(TOP):
            slot = slot_rows[:, route]
            keep = slot >= 0
            where_at = (route_rows[:, route] * CAP + jnp.maximum(slot, 0)).astype(jnp.int32)
            scale = jnp.where(keep, weight_rows[:, route], jnp.zeros((), jnp.float32))
            total = total + scale[:, None] * outputs[where_at]
        results.append(total)
    return jnp.stack(results)
```

```python
import jax
import jax.numpy as jnp
from jax import lax
from jax.experimental import pallas as pl
from jax.experimental.pallas import tpu as pltpu
from jax.sharding import PartitionSpec as P

AXES = ("group", "local")
SIZE = (4, 4, 4, 2)
ORDER = ((2, 1, 0), (0, 1, 2))
META = 128


def flat(place):
    index = 0
    for size, at in zip(SIZE, place):
        index = index * size + at
    return index


def places():
    return [(z, y, x, c) for z in range(4) for y in range(4) for x in range(4) for c in range(2)]


def moved(place, stage, by):
    axis = ORDER[place[3]][stage]
    return tuple((at + by) % 4 if dim == axis else at for dim, at in enumerate(place))


def fetch(block, stage, by):
    return lax.ppermute(block, AXES, [(flat(moved(p, stage, by)), flat(p)) for p in places()])


def send(block, stage, by):
    return lax.ppermute(block, AXES, [(flat(p), flat(moved(p, stage, by))) for p in places()])


def swap(block):
    return lax.ppermute(block, AXES, [(flat(p), flat(p[:3] + (1 - p[3],))) for p in places()])


STEP = 1024


def layer_kernel(first_ref, *refs):
    rows = refs[:8]
    metas = refs[8:16]
    gate, up, shared_gate, shared_up, down, shared_down = refs[16:22]
    own, other = refs[22:24]
    acc_gate, acc_up, acc_sg, acc_su, hid, shared_hid, scale = refs[24:]
    at = pl.program_id(0)
    half = pl.num_programs(0) // 2

    @pl.when(at == 0)
    def _():
        for ref in (acc_gate, acc_up, acc_sg, acc_su):
            ref[...] = jnp.zeros_like(ref)

    @pl.when(at < half)
    def _():
        x = jnp.concatenate([r[...] for r in rows], axis=0)
        for e in range(2):
            acc_gate[e] += jnp.dot(x, gate[e], preferred_element_type=jnp.float32)
            acc_up[e] += jnp.dot(x, up[e], preferred_element_type=jnp.float32)
        dims = (((1,), (1,)), ((), ()))
        acc_sg[...] += lax.dot_general(x, shared_gate[...], dims, preferred_element_type=jnp.float32)
        acc_su[...] += lax.dot_general(x, shared_up[...], dims, preferred_element_type=jnp.float32)

    @pl.when(at == half - 1)
    def _():
        weights = jnp.concatenate([m[...] for m in metas], axis=0).astype(jnp.float32)
        lane = lax.broadcasted_iota(jnp.int32, weights.shape, 1)
        for e in range(2):
            g = acc_gate[e]
            hid[e] = (g / (1.0 + jnp.exp(-g)) * acc_up[e]).astype(jnp.bfloat16)
            mine = jnp.where(lane == first_ref[0, 0] + e, weights, 0.0)
            scale[e] = jnp.broadcast_to(jnp.sum(mine, axis=1, keepdims=True), weights.shape)
        g = acc_sg[...]
        shared_hid[...] = (g / (1.0 + jnp.exp(-g)) * acc_su[...]).astype(jnp.bfloat16)

    @pl.when(at >= half)
    def _():
        total = jnp.dot(shared_hid[...], shared_down[...], preferred_element_type=jnp.float32)
        for e in range(2):
            part = jnp.dot(hid[e], down[e], preferred_element_type=jnp.float32)
            total = total + scale[e][:, :1] * part
        own[...] = total[:128]
        other[...] = total[128:].astype(jnp.bfloat16)


def layer(pieces, first, gate, up, down, shared_gate, shared_up, shared_down):
    width = down.shape[2]
    half = width // STEP
    units = gate.shape[2]
    shared = shared_down.shape[0]
    lead = lambda i: jnp.minimum(i, half - 1)
    trail = lambda i: jnp.maximum(i - half, 0)
    return pl.pallas_call(
        layer_kernel,
        grid=(2 * half,),
        out_shape=(
            jax.ShapeDtypeStruct((128, width), jnp.float32),
            jax.ShapeDtypeStruct((128, width), jnp.bfloat16),
        ),
        in_specs=[pl.BlockSpec(memory_space=pltpu.SMEM)]
        + [pl.BlockSpec((32, STEP), lambda i: (0, lead(i)))] * 8
        + [pl.BlockSpec((32, META), lambda i: (0, width // META))] * 8
        + [pl.BlockSpec((2, STEP, units), lambda i: (0, lead(i), 0))] * 2
        + [pl.BlockSpec((shared, STEP), lambda i: (0, lead(i)))] * 2
        + [
            pl.BlockSpec((2, units, STEP), lambda i: (0, 0, trail(i))),
            pl.BlockSpec((shared, STEP), lambda i: (0, trail(i))),
        ],
        out_specs=[pl.BlockSpec((128, STEP), lambda i: (0, trail(i)))] * 2,
        scratch_shapes=[
            pltpu.VMEM((2, 256, units), jnp.float32),
            pltpu.VMEM((2, 256, units), jnp.float32),
            pltpu.VMEM((256, shared), jnp.float32),
            pltpu.VMEM((256, shared), jnp.float32),
            pltpu.VMEM((2, 256, units), jnp.bfloat16),
            pltpu.VMEM((256, shared), jnp.bfloat16),
            pltpu.VMEM((2, 256, META), jnp.float32),
        ],
        compiler_params=pltpu.CompilerParams(vmem_limit_bytes=32 * 1024 * 1024),
        cost_estimate=pl.CostEstimate(
            flops=6 * 256 * width * (2 * units + shared),
            bytes_accessed=6 * width * (2 * units + shared) + 10 * 128 * width,
            transcendentals=256 * (2 * units + shared),
        ),
        name="layer",
    )(first, *pieces, *pieces, gate, up, shared_gate.T, shared_up.T, down, shared_down)


def body(
    hidden,
    routes,
    slots,
    route_weight,
    expert_gate,
    expert_up,
    expert_down,
    shared_gate,
    shared_up,
    shared_down,
):
    experts = jnp.arange(META, dtype=jnp.int32)
    weight = jnp.where(slots >= 0, route_weight.astype(jnp.float32), 0.0)
    dense = jnp.sum(
        jnp.where(routes[..., None] == experts, weight[..., None], 0.0), axis=2
    )
    block = jnp.concatenate([hidden, dense], axis=2)[:, 0].astype(jnp.bfloat16)

    for stage in range(2):
        block = jnp.concatenate([block] + [fetch(block, stage, by) for by in (1, 3, 2)], axis=0)
    mine = [block] + [fetch(block, 2, by) for by in (1, 3, 2)]
    pieces = mine + [swap(piece) for piece in mine]

    first = (2 * lax.axis_index("group")).astype(jnp.int32).reshape(1, 1)
    own, other = layer(
        pieces, first, expert_gate, expert_up, expert_down, shared_gate, shared_up, shared_down
    )
    total = own + swap(other).astype(jnp.float32)
    for stage, kind in ((2, jnp.bfloat16), (1, jnp.float32), (0, jnp.float32)):
        count = total.shape[0] // 4
        parts = [total[i * count : (i + 1) * count] for i in range(4)]
        got = [send(part.astype(kind), stage, by) for part, by in zip(parts[1:], (1, 3, 2))]
        total = parts[0]
        for part in got:
            total = total + part.astype(jnp.float32)
    return total[:, None, :]


def solution(mesh):
    return jax.shard_map(
        body,
        mesh=mesh,
        in_specs=(
            P(None, ("group", "local"), None),
            P(None, ("group", "local"), None),
            P(None, ("group", "local"), None),
            P(None, ("group", "local"), None),
            P("group", None, "local"),
            P("group", None, "local"),
            P("group", "local", None),
            P(None, ("group", "local")),
            P(None, ("group", "local")),
            P(("group", "local"), None),
        ),
        out_specs=P(None, ("group", "local"), None),
        check_vma=False,
    )
```

```python
import jax
import jax.numpy as jnp
from jax import lax
from jax.experimental import pallas as pl
from jax.experimental.pallas import tpu as pltpu
from jax.sharding import PartitionSpec as P

AXES = ("group", "local")
SIZE = (4, 4, 4, 2)
ORDER = ((2, 1, 0), (1, 0, 2))
META = 128


def flat(place):
    index = 0
    for size, at in zip(SIZE, place):
        index = index * size + at
    return index


def places():
    return [(z, y, x, c) for z in range(4) for y in range(4) for x in range(4) for c in range(2)]


def moved(place, stage, by):
    axis = ORDER[place[3]][stage]
    return tuple((at + by) % 4 if dim == axis else at for dim, at in enumerate(place))


def fetch(block, stage, by):
    return lax.ppermute(block, AXES, [(flat(moved(p, stage, by)), flat(p)) for p in places()])


def send(block, stage, by):
    return lax.ppermute(block, AXES, [(flat(p), flat(moved(p, stage, by))) for p in places()])


def swap(block):
    return lax.ppermute(block, AXES, [(flat(p), flat(p[:3] + (1 - p[3],))) for p in places()])


KSTEP = 3584
NSTEP = 1792
AHEAD = 4


def layer_kernel(first_ref, *refs):
    pieces = refs[:8]
    gate, up, shared_gate, shared_up, down, shared_down = refs[8:14]
    own, other = refs[14:16]
    gate_buf, up_buf, down_buf, sgu_buf, sd_buf, acts, hid, shared_hid, scale, sems = refs[16:]
    width = shared_down.shape[1]
    shared = shared_down.shape[0]
    steps = width // KSTEP
    cuts = width // NSTEP

    loads = []
    for e in range(2):
        for source, target in ((gate, gate_buf), (up, up_buf)):
            for k in range(steps):
                rows = pl.ds(k * KSTEP, KSTEP)
                loads.append((source.at[e, rows], target.at[e, rows]))
        if e == 0:
            loads.append((shared_gate, sgu_buf.at[:shared]))
            loads.append((shared_up, sgu_buf.at[shared:]))
            loads.append((shared_down, sd_buf))
    for n in range(cuts):
        columns = pl.ds(n * NSTEP, NSTEP)
        loads.append((down.at[:, :, columns], down_buf.at[:, :, columns]))
    copies = [pltpu.make_async_copy(s, t, sems.at[i]) for i, (s, t) in enumerate(loads)]
    for copy in copies[:AHEAD]:
        copy.start()
    waited = [0]

    def arrived():
        copies[waited[0]].wait()
        if waited[0] + AHEAD < len(copies):
            copies[waited[0] + AHEAD].start()
        waited[0] += 1

    def rows_of(k, size):
        return jnp.concatenate([p[:, k * size : (k + 1) * size] for p in pieces], axis=0)

    def silu_mul(g, u):
        return (g / (1.0 + jnp.exp(-g)) * u).astype(jnp.bfloat16)

    block = pl.when(first_ref[0, 0] >= 0)

    @block
    def _():
        weights = jnp.concatenate([p[:, width:] for p in pieces], axis=0).astype(jnp.float32)
        lane = lax.broadcasted_iota(jnp.int32, weights.shape, 1)
        for e in range(2):
            mine = jnp.where(lane == first_ref[0, 0] + e, weights, 0.0)
            scale[e] = jnp.broadcast_to(jnp.sum(mine, axis=1, keepdims=True), weights.shape)

    for e in range(2):
        for m, buf in enumerate((gate_buf, up_buf)):
            for k in range(steps):
                arrived()

                @block
                def _(e=e, m=m, k=k, buf=buf):
                    part = jnp.dot(
                        rows_of(k, KSTEP),
                        buf[e, k * KSTEP : (k + 1) * KSTEP],
                        preferred_element_type=jnp.float32,
                    )
                    acts[m] = part if k == 0 else acts[m] + part

        if e == 0:
            arrived()
            arrived()
            arrived()

        @block
        def _(e=e):
            hid[e] = silu_mul(acts[0], acts[1])
            if e == 0:
                dims = (((1,), (1,)), ((), ()))
                both = None
                for k in range(steps):
                    part = lax.dot_general(
                        rows_of(k, KSTEP),
                        sgu_buf[:, k * KSTEP : (k + 1) * KSTEP],
                        dims,
                        preferred_element_type=jnp.float32,
                    )
                    both = part if both is None else both + part
                shared_hid[...] = silu_mul(both[:, :shared], both[:, shared:])

    for n in range(cuts):
        arrived()

        @block
        def _(n=n):
            columns = slice(n * NSTEP, (n + 1) * NSTEP)
            total = jnp.dot(shared_hid[...], sd_buf[:, columns], preferred_element_type=jnp.float32)
            for e in range(2):
                part = jnp.dot(hid[e], down_buf[e, :, columns], preferred_element_type=jnp.float32)
                total = total + scale[e][:, :1] * part
            own[:, columns] = total[:128]
            other[:, columns] = total[128:].astype(jnp.bfloat16)


def layer(pieces, first, gate, up, down, shared_gate, shared_up, shared_down):
    width = down.shape[2]
    units = gate.shape[2]
    shared = shared_down.shape[0]
    vmem = pl.BlockSpec(memory_space=pltpu.VMEM)
    hbm = pl.BlockSpec(memory_space=pl.ANY)
    return pl.pallas_call(
        layer_kernel,
        out_shape=(
            jax.ShapeDtypeStruct((128, width), jnp.float32),
            jax.ShapeDtypeStruct((128, width), jnp.bfloat16),
        ),
        in_specs=[pl.BlockSpec(memory_space=pltpu.SMEM)]
        + [vmem] * 8
        + [hbm] * 6,
        out_specs=[vmem] * 2,
        scratch_shapes=[
            pltpu.VMEM(gate.shape, jnp.bfloat16),
            pltpu.VMEM(up.shape, jnp.bfloat16),
            pltpu.VMEM(down.shape, jnp.bfloat16),
            pltpu.VMEM((2 * shared, width), jnp.bfloat16),
            pltpu.VMEM((shared, width), jnp.bfloat16),
            pltpu.VMEM((2, 256, units), jnp.float32),
            pltpu.VMEM((2, 256, units), jnp.bfloat16),
            pltpu.VMEM((256, shared), jnp.bfloat16),
            pltpu.VMEM((2, 256, META), jnp.float32),
            pltpu.SemaphoreType.DMA((4 * width // KSTEP + 3 + width // NSTEP,)),
        ],
        compiler_params=pltpu.CompilerParams(vmem_limit_bytes=32 * 1024 * 1024),
        cost_estimate=pl.CostEstimate(
            flops=6 * 256 * width * (2 * units + shared),
            bytes_accessed=6 * width * (2 * units + shared) + 10 * 128 * width,
            transcendentals=256 * (2 * units + shared),
        ),
        name="layer",
    )(
        first,
        *pieces,
        *[
            pltpu.with_memory_space_constraint(a, pltpu.HBM)
            for a in (gate, up, shared_gate.T, shared_up.T, down, shared_down)
        ],
    )


def body(
    hidden,
    routes,
    slots,
    route_weight,
    expert_gate,
    expert_up,
    expert_down,
    shared_gate,
    shared_up,
    shared_down,
):
    experts = jnp.arange(META, dtype=jnp.int32)
    weight = jnp.where(slots >= 0, route_weight.astype(jnp.float32), 0.0)
    dense = jnp.sum(
        jnp.where(routes[..., None] == experts, weight[..., None], 0.0), axis=2
    )
    block = jnp.concatenate([hidden, dense], axis=2)[:, 0].astype(jnp.bfloat16)

    for stage in range(2):
        block = jnp.concatenate([block] + [fetch(block, stage, by) for by in (1, 3, 2)], axis=0)
    mine = [block] + [fetch(block, 2, by) for by in (1, 3, 2)]
    pieces = mine + [swap(piece) for piece in mine]

    first = (2 * lax.axis_index("group")).astype(jnp.int32).reshape(1, 1)
    own, other = layer(
        pieces, first, expert_gate, expert_up, expert_down, shared_gate, shared_up, shared_down
    )
    total = own + swap(other).astype(jnp.float32)
    for stage, kind in ((2, jnp.bfloat16), (1, jnp.bfloat16), (0, jnp.float32)):
        count = total.shape[0] // 4
        parts = [total[i * count : (i + 1) * count] for i in range(4)]
        got = [send(part.astype(kind), stage, by) for part, by in zip(parts[1:], (1, 3, 2))]
        total = parts[0]
        for part in got:
            total = total + part.astype(jnp.float32)
    return total[:, None, :]


def solution(mesh):
    return jax.shard_map(
        body,
        mesh=mesh,
        in_specs=(
            P(None, ("group", "local"), None),
            P(None, ("group", "local"), None),
            P(None, ("group", "local"), None),
            P(None, ("group", "local"), None),
            P("group", None, "local"),
            P("group", None, "local"),
            P("group", "local", None),
            P(None, ("group", "local")),
            P(None, ("group", "local")),
            P(("group", "local"), None),
        ),
        out_specs=P(None, ("group", "local"), None),
        check_vma=False,
    )
```

```python
import jax
import jax.numpy as jnp
from jax import lax
from jax.experimental import pallas as pl
from jax.experimental.pallas import tpu as pltpu
from jax.sharding import PartitionSpec as P

AXES = ("group", "local")
SIZE = (4, 4, 4, 2)
ORDER = ((2, 1, 0), (1, 0, 2))
META = 128


def flat(place):
    index = 0
    for size, at in zip(SIZE, place):
        index = index * size + at
    return index


def places():
    return [(z, y, x, c) for z in range(4) for y in range(4) for x in range(4) for c in range(2)]


def moved(place, stage, by):
    axis = ORDER[place[3]][stage]
    return tuple((at + by) % 4 if dim == axis else at for dim, at in enumerate(place))


def fetch(block, stage, by):
    return lax.ppermute(block, AXES, [(flat(moved(p, stage, by)), flat(p)) for p in places()])


def send(block, stage, by):
    return lax.ppermute(block, AXES, [(flat(p), flat(moved(p, stage, by))) for p in places()])


def swap(block):
    return lax.ppermute(block, AXES, [(flat(p), flat(p[:3] + (1 - p[3],))) for p in places()])


KSTEP = 3584
NSTEP = 3584
AHEAD = 4


def layer_kernel(first_ref, *refs):
    pieces = refs[:8]
    gate, up, shared_gate, shared_up, down, shared_down = refs[8:14]
    kept, other = refs[14:16]
    gate_buf, up_buf, down_buf, sgu_buf, acts, hid, sems = refs[16:]
    width = shared_down.shape[1]
    units = down.shape[1]
    shared = shared_down.shape[0]
    steps = width // KSTEP
    cuts = width // NSTEP

    loads = []
    for e in range(2):
        for source, target in ((gate, gate_buf), (up, up_buf)):
            for k in range(steps):
                rows = pl.ds(k * KSTEP, KSTEP)
                loads.append((source.at[e, rows], target.at[e, rows]))
        if e == 0:
            loads.append((shared_gate, sgu_buf.at[:shared]))
            loads.append((shared_up, sgu_buf.at[shared:]))
            loads.append((shared_down, down_buf.at[2 * units :]))
    for n in range(cuts):
        columns = pl.ds(n * NSTEP, NSTEP)
        for e in range(2):
            rows = pl.ds(e * units, units)
            loads.append((down.at[e, :, columns], down_buf.at[rows, columns]))
    copies = [pltpu.make_async_copy(s, t, sems.at[i]) for i, (s, t) in enumerate(loads)]
    for copy in copies[:AHEAD]:
        copy.start()
    waited = [0]

    def arrived():
        copies[waited[0]].wait()
        if waited[0] + AHEAD < len(copies):
            copies[waited[0] + AHEAD].start()
        waited[0] += 1

    def rows_of(k, size):
        return jnp.concatenate([p[:, k * size : (k + 1) * size] for p in pieces], axis=0)

    def silu_mul(g, u):
        return g / (1.0 + jnp.exp(-g)) * u

    block = pl.when(first_ref[0, 0] >= 0)

    for e in range(2):
        for m, buf in enumerate((gate_buf, up_buf)):
            for k in range(steps):
                arrived()

                @block
                def _(e=e, m=m, k=k, buf=buf):
                    part = jnp.dot(
                        rows_of(k, KSTEP),
                        buf[e, k * KSTEP : (k + 1) * KSTEP],
                        preferred_element_type=jnp.float32,
                    )
                    acts[m] = part if k == 0 else acts[m] + part

        if e == 0:
            arrived()
            arrived()
            arrived()

        @block
        def _(e=e):
            weights = jnp.concatenate([p[:, width:] for p in pieces], axis=0).astype(jnp.float32)
            lane = lax.broadcasted_iota(jnp.int32, weights.shape, 1)
            mine = jnp.where(lane == first_ref[0, 0] + e, weights, 0.0)
            scale = jnp.sum(mine, axis=1, keepdims=True)
            act = silu_mul(acts[0], acts[1]) * scale
            hid[:, e * units : (e + 1) * units] = act.astype(jnp.bfloat16)
            if e == 0:
                dims = (((1,), (1,)), ((), ()))
                both = None
                for k in range(steps):
                    part = lax.dot_general(
                        rows_of(k, KSTEP),
                        sgu_buf[:, k * KSTEP : (k + 1) * KSTEP],
                        dims,
                        preferred_element_type=jnp.float32,
                    )
                    both = part if both is None else both + part
                act = silu_mul(both[:, :shared], both[:, shared:])
                hid[:, 2 * units :] = act.astype(jnp.bfloat16)

    for n in range(cuts):
        arrived()
        arrived()

        @block
        def _(n=n):
            columns = slice(n * NSTEP, (n + 1) * NSTEP)
            total = jnp.dot(hid[128:], down_buf[:, columns], preferred_element_type=jnp.float32)
            other[:, columns] = total.astype(jnp.bfloat16)
            if n == 0:
                kept[...] = hid[:128]


def layer(pieces, first, gate, up, down, shared_gate, shared_up, shared_down):
    width = down.shape[2]
    units = gate.shape[2]
    shared = shared_down.shape[0]
    vmem = pl.BlockSpec(memory_space=pltpu.VMEM)
    hbm = pl.BlockSpec(memory_space=pl.ANY)
    return pl.pallas_call(
        layer_kernel,
        out_shape=(
            jax.ShapeDtypeStruct((128, 2 * units + shared), jnp.bfloat16),
            jax.ShapeDtypeStruct((128, width), jnp.bfloat16),
        ),
        in_specs=[pl.BlockSpec(memory_space=pltpu.SMEM)]
        + [vmem] * 8
        + [hbm] * 6,
        out_specs=[vmem] * 2,
        scratch_shapes=[
            pltpu.VMEM(gate.shape, jnp.bfloat16),
            pltpu.VMEM(up.shape, jnp.bfloat16),
            pltpu.VMEM((2 * units + shared, width), jnp.bfloat16),
            pltpu.VMEM((2 * shared, width), jnp.bfloat16),
            pltpu.VMEM((2, 256, units), jnp.float32),
            pltpu.VMEM((256, 2 * units + shared), jnp.bfloat16),
            pltpu.SemaphoreType.DMA((4 * width // KSTEP + 3 + 2 * width // NSTEP,)),
        ],
        compiler_params=pltpu.CompilerParams(vmem_limit_bytes=28 * 1024 * 1024),
        cost_estimate=pl.CostEstimate(
            flops=6 * 256 * width * (2 * units + shared),
            bytes_accessed=6 * width * (2 * units + shared) + 10 * 128 * width,
            transcendentals=256 * (2 * units + shared),
        ),
        name="layer",
    )(
        first,
        *pieces,
        *[
            pltpu.with_memory_space_constraint(a, pltpu.HBM)
            for a in (gate, up, shared_gate.T, shared_up.T, down, shared_down)
        ],
    )


OSTEP = 1792


def down_kernel(hid, down, shared_down, out, buf, sems):
    units, width = down.shape[1:]
    cuts = width // OSTEP
    copies = [pltpu.make_async_copy(shared_down, buf.at[2 * units :], sems.at[0])]
    for n in range(cuts):
        columns = pl.ds(n * OSTEP, OSTEP)
        for e in range(2):
            rows = pl.ds(e * units, units)
            copies.append(
                pltpu.make_async_copy(
                    down.at[e, :, columns], buf.at[rows, columns], sems.at[1 + 2 * n + e]
                )
            )
    for copy in copies:
        copy.start()
    copies[0].wait()
    for n in range(cuts):
        copies[1 + 2 * n].wait()
        copies[2 + 2 * n].wait()

        @pl.when(pl.program_id(0) >= 0)
        def _(n=n):
            columns = slice(n * OSTEP, (n + 1) * OSTEP)
            out[:, columns] = jnp.dot(
                hid[...], buf[:, columns], preferred_element_type=jnp.float32
            )


def down_own(hid, down, shared_down):
    units, width = down.shape[1:]
    shared = shared_down.shape[0]
    vmem = pl.BlockSpec(memory_space=pltpu.VMEM)
    hbm = pl.BlockSpec(memory_space=pl.ANY)
    return pl.pallas_call(
        down_kernel,
        grid=(1,),
        out_shape=jax.ShapeDtypeStruct((128, width), jnp.float32),
        in_specs=[vmem, hbm, hbm],
        out_specs=vmem,
        scratch_shapes=[
            pltpu.VMEM((2 * units + shared, width), jnp.bfloat16),
            pltpu.SemaphoreType.DMA((1 + 2 * width // OSTEP,)),
        ],
        compiler_params=pltpu.CompilerParams(vmem_limit_bytes=16 * 1024 * 1024),
        cost_estimate=pl.CostEstimate(
            flops=2 * 128 * width * (2 * units + shared),
            bytes_accessed=2 * width * (2 * units + shared) + 4 * 128 * width,
            transcendentals=0,
        ),
        name="down",
    )(hid, *[pltpu.with_memory_space_constraint(a, pltpu.HBM) for a in (down, shared_down)])


def prepare_kernel(hidden, routes, slots, weight, out):
    width = hidden.shape[2]
    out[:, :width] = jnp.concatenate([hidden[0], hidden[1]], axis=0).astype(jnp.bfloat16)
    experts = jnp.concatenate([routes[0], routes[1]], axis=0)
    kept = jnp.concatenate([slots[0], slots[1]], axis=0) >= 0
    weights = jnp.where(kept, weight[...].astype(jnp.float32), 0.0)
    lane = lax.broadcasted_iota(jnp.int32, (2, META), 1)
    dense = jnp.zeros((2, META), jnp.float32)
    for k in range(experts.shape[1]):
        dense += jnp.where(lane == experts[:, k : k + 1], weights[:, k : k + 1], 0.0)
    out[:, width:] = dense.astype(jnp.bfloat16)


def prepare(hidden, routes, slots, route_weight):
    steps, _, width = hidden.shape
    return pl.pallas_call(
        prepare_kernel,
        out_shape=pltpu.VMEM((steps, width + META), jnp.bfloat16),
        name="prepare",
    )(hidden, routes, slots, route_weight[:, 0])


def body(
    hidden,
    routes,
    slots,
    route_weight,
    expert_gate,
    expert_up,
    expert_down,
    shared_gate,
    shared_up,
    shared_down,
):
    block = prepare(hidden, routes, slots, route_weight)
    for stage in range(2):
        block = jnp.concatenate([block] + [fetch(block, stage, by) for by in (1, 3, 2)], axis=0)
    mine = [block] + [fetch(block, 2, by) for by in (1, 3, 2)]
    pieces = mine + [swap(piece) for piece in mine]

    first = (2 * lax.axis_index("group")).astype(jnp.int32).reshape(1, 1)
    kept, other = layer(
        pieces, first, expert_gate, expert_up, expert_down, shared_gate, shared_up, shared_down
    )
    other = swap(other)
    total = down_own(kept, expert_down, shared_down) + other.astype(jnp.float32)
    for stage, kind in ((2, jnp.bfloat16), (1, jnp.bfloat16), (0, jnp.float32)):
        count = total.shape[0] // 4
        parts = [total[i * count : (i + 1) * count] for i in range(4)]
        got = [send(part.astype(kind), stage, by) for part, by in zip(parts[1:], (1, 3, 2))]
        total = parts[0]
        for part in got:
            total = total + part.astype(jnp.float32)
    return total[:, None, :]


def solution(mesh):
    return jax.shard_map(
        body,
        mesh=mesh,
        in_specs=(
            P(None, ("group", "local"), None),
            P(None, ("group", "local"), None),
            P(None, ("group", "local"), None),
            P(None, ("group", "local"), None),
            P("group", None, "local"),
            P("group", None, "local"),
            P("group", "local", None),
            P(None, ("group", "local")),
            P(None, ("group", "local")),
            P(("group", "local"), None),
        ),
        out_specs=P(None, ("group", "local"), None),
        check_vma=False,
    )
```

```python
import jax
import jax.numpy as jnp
from jax import lax
from jax.experimental import pallas as pl
from jax.experimental.pallas import tpu as pltpu
from jax.sharding import PartitionSpec as P

AXES = ("group", "local")
SIZE = (4, 4, 4, 2)
ORDER = ((2, 1, 0), (1, 0, 2))
META = 128


def flat(place):
    index = 0
    for size, at in zip(SIZE, place):
        index = index * size + at
    return index


def places():
    return [(z, y, x, c) for z in range(4) for y in range(4) for x in range(4) for c in range(2)]


def moved(place, stage, by):
    axis = ORDER[place[3]][stage]
    return tuple((at + by) % 4 if dim == axis else at for dim, at in enumerate(place))


def fetch(block, stage, by):
    return lax.ppermute(block, AXES, [(flat(moved(p, stage, by)), flat(p)) for p in places()])


def send(block, stage, by):
    return lax.ppermute(block, AXES, [(flat(p), flat(moved(p, stage, by))) for p in places()])


def swap(block):
    return lax.ppermute(block, AXES, [(flat(p), flat(p[:3] + (1 - p[3],))) for p in places()])


SPLIT = 4
NSTEP = 3584
AHEAD = 12


def layer_kernel(first_ref, *refs):
    pieces = refs[:8]
    gate, up, shared_gate, shared_up, down, shared_down = refs[8:14]
    kept, other = refs[14:16]
    gate_buf, up_buf, down_buf, sgu_buf, acts, hid, sems = refs[16:]
    units, width = down.shape[1:]
    shared = shared_down.shape[0]
    cuts = width // NSTEP

    groups = [[(shared_gate, sgu_buf.at[:shared]), (shared_up, sgu_buf.at[shared:])]]
    for e in range(2):
        for source, target in ((gate, gate_buf), (up, up_buf)):
            size = width // SPLIT
            parts = [pl.ds(i * size, size) for i in range(SPLIT)]
            groups.append([(source.at[e, rows], target.at[e, rows]) for rows in parts])
    for n in range(cuts):
        columns = pl.ds(n * NSTEP, NSTEP)
        group = [(shared_down, down_buf.at[2 * units :])] if n == 0 else []
        for e in range(2):
            size = 2 * units // SPLIT
            for i in range(SPLIT // 2):
                rows = pl.ds(e * units + i * size, size)
                group.append(
                    (down.at[e, pl.ds(i * size, size), columns], down_buf.at[rows, columns])
                )
        groups.append(group)
    loads = [load for group in groups for load in group]
    copies = [pltpu.make_async_copy(s, t, sems.at[i]) for i, (s, t) in enumerate(loads)]
    for copy in copies[:AHEAD]:
        copy.start()
    waited = [0, 0]

    def arrived():
        for _ in groups[waited[0]]:
            copies[waited[1]].wait()
            if waited[1] + AHEAD < len(copies):
                copies[waited[1] + AHEAD].start()
            waited[1] += 1
        waited[0] += 1

    def rows_of():
        return jnp.concatenate([p[:, :width] for p in pieces], axis=0)

    def silu_mul(g, u):
        return g / (1.0 + jnp.exp(-g)) * u

    block = pl.when(first_ref[0, 0] >= 0)

    arrived()

    @block
    def _():
        both = lax.dot_general(
            rows_of(), sgu_buf[...], (((1,), (1,)), ((), ())), preferred_element_type=jnp.float32
        )
        act = silu_mul(both[:, :shared], both[:, shared:])
        hid[:, 2 * units :] = act.astype(jnp.bfloat16)

    for e in range(2):
        arrived()

        @block
        def _(e=e):
            acts[...] = jnp.dot(rows_of(), gate_buf[e], preferred_element_type=jnp.float32)

        arrived()

        @block
        def _(e=e):
            up_act = jnp.dot(rows_of(), up_buf[e], preferred_element_type=jnp.float32)
            weights = jnp.concatenate([p[:, width:] for p in pieces], axis=0).astype(jnp.float32)
            lane = lax.broadcasted_iota(jnp.int32, weights.shape, 1)
            mine = jnp.where(lane == first_ref[0, 0] + e, weights, 0.0)
            scale = jnp.sum(mine, axis=1, keepdims=True)
            act = silu_mul(acts[...], up_act) * scale
            hid[:, e * units : (e + 1) * units] = act.astype(jnp.bfloat16)

    for n in range(cuts):
        arrived()

        @block
        def _(n=n):
            columns = slice(n * NSTEP, (n + 1) * NSTEP)
            total = jnp.dot(hid[128:], down_buf[:, columns], preferred_element_type=jnp.float32)
            other[:, columns] = total.astype(jnp.bfloat16)
            if n == 0:
                kept[...] = hid[:128]


def layer(pieces, first, gate, up, down, shared_gate, shared_up, shared_down):
    width = down.shape[2]
    units = gate.shape[2]
    shared = shared_down.shape[0]
    vmem = pl.BlockSpec(memory_space=pltpu.VMEM)
    hbm = pl.BlockSpec(memory_space=pl.ANY)
    return pl.pallas_call(
        layer_kernel,
        out_shape=(
            jax.ShapeDtypeStruct((128, 2 * units + shared), jnp.bfloat16),
            jax.ShapeDtypeStruct((128, width), jnp.bfloat16),
        ),
        in_specs=[pl.BlockSpec(memory_space=pltpu.SMEM)]
        + [vmem] * 8
        + [hbm] * 6,
        out_specs=[vmem] * 2,
        scratch_shapes=[
            pltpu.VMEM(gate.shape, jnp.bfloat16),
            pltpu.VMEM(up.shape, jnp.bfloat16),
            pltpu.VMEM((2 * units + shared, width), jnp.bfloat16),
            pltpu.VMEM((2 * shared, width), jnp.bfloat16),
            pltpu.VMEM((256, units), jnp.float32),
            pltpu.VMEM((256, 2 * units + shared), jnp.bfloat16),
            pltpu.SemaphoreType.DMA((3 + SPLIT * (4 + width // NSTEP),)),
        ],
        compiler_params=pltpu.CompilerParams(vmem_limit_bytes=28 * 1024 * 1024),
        cost_estimate=pl.CostEstimate(
            flops=6 * 256 * width * (2 * units + shared),
            bytes_accessed=6 * width * (2 * units + shared) + 10 * 128 * width,
            transcendentals=256 * (2 * units + shared),
        ),
        name="layer",
    )(
        first,
        *pieces,
        *[
            pltpu.with_memory_space_constraint(a, pltpu.HBM)
            for a in (gate, up, shared_gate.T, shared_up.T, down, shared_down)
        ],
    )


OSTEP = 1792


def down_kernel(hid, down, shared_down, out, buf, sems):
    units, width = down.shape[1:]
    cuts = width // OSTEP
    copies = [pltpu.make_async_copy(shared_down, buf.at[2 * units :], sems.at[0])]
    for n in range(cuts):
        columns = pl.ds(n * OSTEP, OSTEP)
        for e in range(2):
            rows = pl.ds(e * units, units)
            copies.append(
                pltpu.make_async_copy(
                    down.at[e, :, columns], buf.at[rows, columns], sems.at[1 + 2 * n + e]
                )
            )
    for copy in copies:
        copy.start()
    copies[0].wait()
    for n in range(cuts):
        copies[1 + 2 * n].wait()
        copies[2 + 2 * n].wait()

        @pl.when(pl.program_id(0) >= 0)
        def _(n=n):
            columns = slice(n * OSTEP, (n + 1) * OSTEP)
            out[:, columns] = jnp.dot(
                hid[...], buf[:, columns], preferred_element_type=jnp.float32
            )


def down_own(hid, down, shared_down):
    units, width = down.shape[1:]
    shared = shared_down.shape[0]
    vmem = pl.BlockSpec(memory_space=pltpu.VMEM)
    hbm = pl.BlockSpec(memory_space=pl.ANY)
    return pl.pallas_call(
        down_kernel,
        grid=(1,),
        out_shape=jax.ShapeDtypeStruct((128, width), jnp.float32),
        in_specs=[vmem, hbm, hbm],
        out_specs=vmem,
        scratch_shapes=[
            pltpu.VMEM((2 * units + shared, width), jnp.bfloat16),
            pltpu.SemaphoreType.DMA((1 + 2 * width // OSTEP,)),
        ],
        compiler_params=pltpu.CompilerParams(vmem_limit_bytes=16 * 1024 * 1024),
        cost_estimate=pl.CostEstimate(
            flops=2 * 128 * width * (2 * units + shared),
            bytes_accessed=2 * width * (2 * units + shared) + 4 * 128 * width,
            transcendentals=0,
        ),
        name="down",
    )(hid, *[pltpu.with_memory_space_constraint(a, pltpu.HBM) for a in (down, shared_down)])


def prepare_kernel(hidden, routes, slots, weight, out):
    width = hidden.shape[2]
    out[:, :width] = jnp.concatenate([hidden[0], hidden[1]], axis=0).astype(jnp.bfloat16)
    experts = jnp.concatenate([routes[0], routes[1]], axis=0)
    kept = jnp.concatenate([slots[0], slots[1]], axis=0) >= 0
    weights = jnp.where(kept, weight[...].astype(jnp.float32), 0.0)
    lane = lax.broadcasted_iota(jnp.int32, (2, META), 1)
    dense = jnp.zeros((2, META), jnp.float32)
    for k in range(experts.shape[1]):
        dense += jnp.where(lane == experts[:, k : k + 1], weights[:, k : k + 1], 0.0)
    out[:, width:] = dense.astype(jnp.bfloat16)


def prepare(hidden, routes, slots, route_weight):
    steps, _, width = hidden.shape
    return pl.pallas_call(
        prepare_kernel,
        out_shape=pltpu.VMEM((steps, width + META), jnp.bfloat16),
        name="prepare",
    )(hidden, routes, slots, route_weight[:, 0])


def body(
    hidden,
    routes,
    slots,
    route_weight,
    expert_gate,
    expert_up,
    expert_down,
    shared_gate,
    shared_up,
    shared_down,
):
    block = prepare(hidden, routes, slots, route_weight)
    for stage in range(2):
        block = jnp.concatenate([block] + [fetch(block, stage, by) for by in (1, 3, 2)], axis=0)
    mine = [block] + [fetch(block, 2, by) for by in (1, 3, 2)]
    pieces = mine + [swap(piece) for piece in mine]

    first = (2 * lax.axis_index("group")).astype(jnp.int32).reshape(1, 1)
    kept, other = layer(
        pieces, first, expert_gate, expert_up, expert_down, shared_gate, shared_up, shared_down
    )
    other = swap(other)
    total = down_own(kept, expert_down, shared_down) + other.astype(jnp.float32)
    for stage, kind in ((2, jnp.bfloat16), (1, jnp.bfloat16), (0, jnp.float32)):
        count = total.shape[0] // 4
        parts = [total[i * count : (i + 1) * count] for i in range(4)]
        got = [send(part.astype(kind), stage, by) for part, by in zip(parts[:0:-1], (2, 3, 1))]
        total = parts[0]
        for part in got:
            total = total + part.astype(jnp.float32)
    return total[:, None, :]


def solution(mesh):
    return jax.shard_map(
        body,
        mesh=mesh,
        in_specs=(
            P(None, ("group", "local"), None),
            P(None, ("group", "local"), None),
            P(None, ("group", "local"), None),
            P(None, ("group", "local"), None),
            P("group", None, "local"),
            P("group", None, "local"),
            P("group", "local", None),
            P(None, ("group", "local")),
            P(None, ("group", "local")),
            P(("group", "local"), None),
        ),
        out_specs=P(None, ("group", "local"), None),
        check_vma=False,
    )
```

```python
import jax
import jax.numpy as jnp
from jax import lax
from jax.experimental import pallas as pl
from jax.experimental.pallas import tpu as pltpu
from jax.sharding import PartitionSpec as P

AXES = ("group", "local")
SIZE = (4, 4, 4, 2)
ORDER = ((2, 1, 0), (1, 0, 2))
META = 128


def flat(place):
    index = 0
    for size, at in zip(SIZE, place):
        index = index * size + at
    return index


def places():
    return [(z, y, x, c) for z in range(4) for y in range(4) for x in range(4) for c in range(2)]


def moved(place, stage, by):
    axis = ORDER[place[3]][stage]
    return tuple((at + by) % 4 if dim == axis else at for dim, at in enumerate(place))


def fetch(block, stage, by):
    return lax.ppermute(block, AXES, [(flat(moved(p, stage, by)), flat(p)) for p in places()])


def send(block, stage, by):
    return lax.ppermute(block, AXES, [(flat(p), flat(moved(p, stage, by))) for p in places()])


def swap(block):
    return lax.ppermute(block, AXES, [(flat(p), flat(p[:3] + (1 - p[3],))) for p in places()])


SPLIT = 4
NSTEP = 3584
AHEAD = 12


def layer_kernel(first_ref, *refs):
    pieces = refs[:8]
    gate, up, shared_gate, shared_up, down, shared_down = refs[8:14]
    kept, other = refs[14:16]
    gate_buf, up_buf, down_buf, sgu_buf, acts, hid, sems = refs[16:]
    units, width = down.shape[1:]
    shared = shared_down.shape[0]
    cuts = width // NSTEP

    groups = [[(shared_gate, sgu_buf.at[:shared]), (shared_up, sgu_buf.at[shared:])]]
    for e in range(2):
        for source, target in ((gate, gate_buf), (up, up_buf)):
            size = width // SPLIT
            parts = [pl.ds(i * size, size) for i in range(SPLIT)]
            groups.append([(source.at[e, rows], target.at[e, rows]) for rows in parts])
    for n in range(cuts):
        columns = pl.ds(n * NSTEP, NSTEP)
        group = [(shared_down, down_buf.at[2 * units :])] if n == 0 else []
        for e in range(2):
            size = 2 * units // SPLIT
            for i in range(SPLIT // 2):
                rows = pl.ds(e * units + i * size, size)
                group.append(
                    (down.at[e, pl.ds(i * size, size), columns], down_buf.at[rows, columns])
                )
        groups.append(group)
    loads = [load for group in groups for load in group]
    copies = [pltpu.make_async_copy(s, t, sems.at[i]) for i, (s, t) in enumerate(loads)]
    for copy in copies[:AHEAD]:
        copy.start()
    waited = [0, 0]

    def arrived():
        for _ in groups[waited[0]]:
            copies[waited[1]].wait()
            if waited[1] + AHEAD < len(copies):
                copies[waited[1] + AHEAD].start()
            waited[1] += 1
        waited[0] += 1

    def rows_of():
        return jnp.concatenate([p[:, :width] for p in pieces], axis=0)

    def silu_mul(g, u):
        return g / (1.0 + jnp.exp(-g)) * u

    block = pl.when(first_ref[0, 0] >= 0)

    arrived()

    @block
    def _():
        both = lax.dot_general(
            rows_of(), sgu_buf[...], (((1,), (1,)), ((), ())), preferred_element_type=jnp.float32
        )
        act = silu_mul(both[:, :shared], both[:, shared:])
        hid[:, 2 * units :] = act.astype(jnp.bfloat16)

    for e in range(2):
        arrived()

        @block
        def _(e=e):
            acts[...] = jnp.dot(rows_of(), gate_buf[e], preferred_element_type=jnp.float32)

        arrived()

        @block
        def _(e=e):
            up_act = jnp.dot(rows_of(), up_buf[e], preferred_element_type=jnp.float32)
            weights = jnp.concatenate([p[:, width:] for p in pieces], axis=0).astype(jnp.float32)
            lane = lax.broadcasted_iota(jnp.int32, weights.shape, 1)
            mine = jnp.where(lane == first_ref[0, 0] + e, weights, 0.0)
            scale = jnp.sum(mine, axis=1, keepdims=True)
            act = silu_mul(acts[...], up_act) * scale
            hid[:, e * units : (e + 1) * units] = act.astype(jnp.bfloat16)

    for n in range(cuts):
        arrived()

        @block
        def _(n=n):
            columns = slice(n * NSTEP, (n + 1) * NSTEP)
            total = jnp.dot(hid[128:], down_buf[:, columns], preferred_element_type=jnp.float32)
            other[:, columns] = total.astype(jnp.bfloat16)
            if n == 0:
                kept[...] = hid[:128]


def layer(pieces, first, gate, up, down, shared_gate, shared_up, shared_down):
    width = down.shape[2]
    units = gate.shape[2]
    shared = shared_down.shape[0]
    vmem = pl.BlockSpec(memory_space=pltpu.VMEM)
    hbm = pl.BlockSpec(memory_space=pl.ANY)
    return pl.pallas_call(
        layer_kernel,
        out_shape=(
            jax.ShapeDtypeStruct((128, 2 * units + shared), jnp.bfloat16),
            jax.ShapeDtypeStruct((128, width), jnp.bfloat16),
        ),
        in_specs=[pl.BlockSpec(memory_space=pltpu.SMEM)]
        + [vmem] * 8
        + [hbm] * 6,
        out_specs=[vmem] * 2,
        scratch_shapes=[
            pltpu.VMEM(gate.shape, jnp.bfloat16),
            pltpu.VMEM(up.shape, jnp.bfloat16),
            pltpu.VMEM((2 * units + shared, width), jnp.bfloat16),
            pltpu.VMEM((2 * shared, width), jnp.bfloat16),
            pltpu.VMEM((256, units), jnp.float32),
            pltpu.VMEM((256, 2 * units + shared), jnp.bfloat16),
            pltpu.SemaphoreType.DMA((3 + SPLIT * (4 + width // NSTEP),)),
        ],
        compiler_params=pltpu.CompilerParams(vmem_limit_bytes=28 * 1024 * 1024),
        cost_estimate=pl.CostEstimate(
            flops=6 * 256 * width * (2 * units + shared),
            bytes_accessed=6 * width * (2 * units + shared) + 10 * 128 * width,
            transcendentals=256 * (2 * units + shared),
        ),
        name="layer",
    )(
        first,
        *pieces,
        *[
            pltpu.with_memory_space_constraint(a, pltpu.HBM)
            for a in (gate, up, shared_gate.T, shared_up.T, down, shared_down)
        ],
    )


OSTEP = 1792


def down_kernel(hid, down, shared_down, out, buf, sems):
    units, width = down.shape[1:]
    cuts = width // OSTEP
    copies = [pltpu.make_async_copy(shared_down, buf.at[2 * units :], sems.at[0])]
    for n in range(cuts):
        columns = pl.ds(n * OSTEP, OSTEP)
        for e in range(2):
            rows = pl.ds(e * units, units)
            copies.append(
                pltpu.make_async_copy(
                    down.at[e, :, columns], buf.at[rows, columns], sems.at[1 + 2 * n + e]
                )
            )
    for copy in copies:
        copy.start()
    copies[0].wait()
    for n in range(cuts):
        copies[1 + 2 * n].wait()
        copies[2 + 2 * n].wait()

        @pl.when(pl.program_id(0) >= 0)
        def _(n=n):
            columns = slice(n * OSTEP, (n + 1) * OSTEP)
            out[:, columns] = jnp.dot(
                hid[...], buf[:, columns], preferred_element_type=jnp.float32
            )


def down_own(hid, down, shared_down):
    units, width = down.shape[1:]
    shared = shared_down.shape[0]
    vmem = pl.BlockSpec(memory_space=pltpu.VMEM)
    hbm = pl.BlockSpec(memory_space=pl.ANY)
    return pl.pallas_call(
        down_kernel,
        grid=(1,),
        out_shape=jax.ShapeDtypeStruct((128, width), jnp.float32),
        in_specs=[vmem, hbm, hbm],
        out_specs=vmem,
        scratch_shapes=[
            pltpu.VMEM((2 * units + shared, width), jnp.bfloat16),
            pltpu.SemaphoreType.DMA((1 + 2 * width // OSTEP,)),
        ],
        compiler_params=pltpu.CompilerParams(vmem_limit_bytes=16 * 1024 * 1024),
        cost_estimate=pl.CostEstimate(
            flops=2 * 128 * width * (2 * units + shared),
            bytes_accessed=2 * width * (2 * units + shared) + 4 * 128 * width,
            transcendentals=0,
        ),
        name="down",
    )(hid, *[pltpu.with_memory_space_constraint(a, pltpu.HBM) for a in (down, shared_down)])


def prepare_kernel(hidden, routes, slots, weight, out):
    width = hidden.shape[2]
    out[:, :width] = jnp.concatenate([hidden[0], hidden[1]], axis=0).astype(jnp.bfloat16)
    experts = jnp.concatenate([routes[0], routes[1]], axis=0)
    kept = jnp.concatenate([slots[0], slots[1]], axis=0) >= 0
    weights = jnp.where(kept, weight[...].astype(jnp.float32), 0.0)
    lane = lax.broadcasted_iota(jnp.int32, (2, META), 1)
    dense = jnp.zeros((2, META), jnp.float32)
    for k in range(experts.shape[1]):
        dense += jnp.where(lane == experts[:, k : k + 1], weights[:, k : k + 1], 0.0)
    out[:, width:] = dense.astype(jnp.bfloat16)


def prepare(hidden, routes, slots, route_weight):
    steps, _, width = hidden.shape
    return pl.pallas_call(
        prepare_kernel,
        out_shape=pltpu.VMEM((steps, width + META), jnp.bfloat16),
        name="prepare",
    )(hidden, routes, slots, route_weight[:, 0])


def body(
    hidden,
    routes,
    slots,
    route_weight,
    expert_gate,
    expert_up,
    expert_down,
    shared_gate,
    shared_up,
    shared_down,
):
    block = prepare(hidden, routes, slots, route_weight)
    for stage in range(2):
        block = jnp.concatenate([block] + [fetch(block, stage, by) for by in (1, 3, 2)], axis=0)
    mine = [block] + [fetch(block, 2, by) for by in (1, 3, 2)]
    pieces = mine + [swap(piece) for piece in mine]

    first = (2 * lax.axis_index("group")).astype(jnp.int32).reshape(1, 1)
    kept, other = layer(
        pieces, first, expert_gate, expert_up, expert_down, shared_gate, shared_up, shared_down
    )
    other = swap(other)
    total = down_own(kept, expert_down, shared_down) + other.astype(jnp.float32)
    for stage, kind in ((2, jnp.bfloat16), (1, jnp.bfloat16), (0, jnp.bfloat16)):
        count = total.shape[0] // 4
        parts = [total[i * count : (i + 1) * count] for i in range(4)]
        got = [send(part.astype(kind), stage, by) for part, by in zip(parts[:0:-1], (2, 3, 1))]
        total = parts[0]
        for part in got:
            total = total + part.astype(jnp.float32)
    return total[:, None, :]


def solution(mesh):
    return jax.shard_map(
        body,
        mesh=mesh,
        in_specs=(
            P(None, ("group", "local"), None),
            P(None, ("group", "local"), None),
            P(None, ("group", "local"), None),
            P(None, ("group", "local"), None),
            P("group", None, "local"),
            P("group", None, "local"),
            P("group", "local", None),
            P(None, ("group", "local")),
            P(None, ("group", "local")),
            P(("group", "local"), None),
        ),
        out_specs=P(None, ("group", "local"), None),
        check_vma=False,
    )
```

```python
import jax
import jax.numpy as jnp
from jax import lax
from jax.experimental import pallas as pl
from jax.experimental.pallas import tpu as pltpu
from jax.sharding import PartitionSpec as P

AXES = ("group", "local")
SIZE = (4, 4, 4, 2)
ORDER = ((2, 1, 0), (1, 0, 2))
META = 128


def flat(place):
    index = 0
    for size, at in zip(SIZE, place):
        index = index * size + at
    return index


def places():
    return [(z, y, x, c) for z in range(4) for y in range(4) for x in range(4) for c in range(2)]


def moved(place, stage, by):
    axis = ORDER[place[3]][stage]
    return tuple((at + by) % 4 if dim == axis else at for dim, at in enumerate(place))


def fetch(block, stage, by):
    return lax.ppermute(block, AXES, [(flat(moved(p, stage, by)), flat(p)) for p in places()])


def send(block, stage, by):
    return lax.ppermute(block, AXES, [(flat(p), flat(moved(p, stage, by))) for p in places()])


def swap(block):
    return lax.ppermute(block, AXES, [(flat(p), flat(p[:3] + (1 - p[3],))) for p in places()])


SPLIT = 4
NSTEP = 3584
AHEAD = 12


def layer_kernel(first_ref, *refs):
    pieces = refs[:8]
    gate, up, shared_gate, shared_up, down, shared_down = refs[8:14]
    kept, other = refs[14:16]
    gate_buf, up_buf, down_buf, sgu_buf, acts, hid, sems = refs[16:]
    units, width = down.shape[1:]
    shared = shared_down.shape[0]
    cuts = width // NSTEP

    groups = [[(shared_gate, sgu_buf.at[:shared]), (shared_up, sgu_buf.at[shared:])]]
    for e in range(2):
        for source, target in ((gate, gate_buf), (up, up_buf)):
            size = width // SPLIT
            parts = [pl.ds(i * size, size) for i in range(SPLIT)]
            groups.append([(source.at[e, rows], target.at[e, rows]) for rows in parts])
    for n in range(cuts):
        columns = pl.ds(n * NSTEP, NSTEP)
        group = [(shared_down, down_buf.at[2 * units :])] if n == 0 else []
        for e in range(2):
            size = 2 * units // SPLIT
            for i in range(SPLIT // 2):
                rows = pl.ds(e * units + i * size, size)
                group.append(
                    (down.at[e, pl.ds(i * size, size), columns], down_buf.at[rows, columns])
                )
        groups.append(group)
    loads = [load for group in groups for load in group]
    copies = [pltpu.make_async_copy(s, t, sems.at[i]) for i, (s, t) in enumerate(loads)]
    for copy in copies[:AHEAD]:
        copy.start()
    waited = [0, 0]

    def arrived():
        for _ in groups[waited[0]]:
            copies[waited[1]].wait()
            if waited[1] + AHEAD < len(copies):
                copies[waited[1] + AHEAD].start()
            waited[1] += 1
        waited[0] += 1

    def rows_of():
        return jnp.concatenate([p[:, :width] for p in pieces], axis=0)

    def silu_mul(g, u):
        return g / (1.0 + jnp.exp(-g)) * u

    block = pl.when(first_ref[0, 0] >= 0)

    arrived()

    @block
    def _():
        both = lax.dot_general(
            rows_of(), sgu_buf[...], (((1,), (1,)), ((), ())), preferred_element_type=jnp.float32
        )
        act = silu_mul(both[:, :shared], both[:, shared:])
        hid[:, 2 * units :] = act.astype(jnp.bfloat16)

    for e in range(2):
        arrived()

        @block
        def _(e=e):
            acts[...] = jnp.dot(rows_of(), gate_buf[e], preferred_element_type=jnp.float32)

        arrived()

        @block
        def _(e=e):
            up_act = jnp.dot(rows_of(), up_buf[e], preferred_element_type=jnp.float32)
            weights = jnp.concatenate([p[:, width:] for p in pieces], axis=0).astype(jnp.float32)
            lane = lax.broadcasted_iota(jnp.int32, weights.shape, 1)
            mine = jnp.where(lane == first_ref[0, 0] + e, weights, 0.0)
            scale = jnp.sum(mine, axis=1, keepdims=True)
            act = silu_mul(acts[...], up_act) * scale
            hid[:, e * units : (e + 1) * units] = act.astype(jnp.bfloat16)

    for n in range(cuts):
        arrived()

        @block
        def _(n=n):
            columns = slice(n * NSTEP, (n + 1) * NSTEP)
            total = jnp.dot(hid[128:], down_buf[:, columns], preferred_element_type=jnp.float32)
            other[:, columns] = total.astype(jnp.bfloat16)
            if n == 0:
                kept[...] = hid[:128]


def layer(pieces, first, gate, up, down, shared_gate, shared_up, shared_down):
    width = down.shape[2]
    units = gate.shape[2]
    shared = shared_down.shape[0]
    vmem = pl.BlockSpec(memory_space=pltpu.VMEM)
    hbm = pl.BlockSpec(memory_space=pl.ANY)
    return pl.pallas_call(
        layer_kernel,
        out_shape=(
            jax.ShapeDtypeStruct((128, 2 * units + shared), jnp.bfloat16),
            jax.ShapeDtypeStruct((128, width), jnp.bfloat16),
        ),
        in_specs=[pl.BlockSpec(memory_space=pltpu.SMEM)]
        + [vmem] * 8
        + [hbm] * 6,
        out_specs=[vmem] * 2,
        scratch_shapes=[
            pltpu.VMEM(gate.shape, jnp.bfloat16),
            pltpu.VMEM(up.shape, jnp.bfloat16),
            pltpu.VMEM((2 * units + shared, width), jnp.bfloat16),
            pltpu.VMEM((2 * shared, width), jnp.bfloat16),
            pltpu.VMEM((256, units), jnp.float32),
            pltpu.VMEM((256, 2 * units + shared), jnp.bfloat16),
            pltpu.SemaphoreType.DMA((3 + SPLIT * (4 + width // NSTEP),)),
        ],
        compiler_params=pltpu.CompilerParams(vmem_limit_bytes=28 * 1024 * 1024),
        cost_estimate=pl.CostEstimate(
            flops=6 * 256 * width * (2 * units + shared),
            bytes_accessed=6 * width * (2 * units + shared) + 10 * 128 * width,
            transcendentals=256 * (2 * units + shared),
        ),
        name="layer",
    )(
        first,
        *pieces,
        *[
            pltpu.with_memory_space_constraint(a, pltpu.HBM)
            for a in (gate, up, shared_gate.T, shared_up.T, down, shared_down)
        ],
    )


OSTEP = 1024


def down_kernel(hid, down, shared_down, out, buf, sems):
    units, width = down.shape[1:]
    cuts = width // OSTEP
    copies = [pltpu.make_async_copy(shared_down, buf.at[2 * units :], sems.at[0])]
    for n in range(cuts):
        columns = pl.ds(n * OSTEP, OSTEP)
        for e in range(2):
            rows = pl.ds(e * units, units)
            copies.append(
                pltpu.make_async_copy(
                    down.at[e, :, columns], buf.at[rows, columns], sems.at[1 + 2 * n + e]
                )
            )
    for copy in copies:
        copy.start()
    copies[0].wait()
    for n in range(cuts):
        copies[1 + 2 * n].wait()
        copies[2 + 2 * n].wait()

        @pl.when(pl.program_id(0) >= 0)
        def _(n=n):
            columns = slice(n * OSTEP, (n + 1) * OSTEP)
            out[:, columns] = jnp.dot(
                hid[...], buf[:, columns], preferred_element_type=jnp.float32
            )


def down_own(hid, down, shared_down):
    units, width = down.shape[1:]
    shared = shared_down.shape[0]
    vmem = pl.BlockSpec(memory_space=pltpu.VMEM)
    hbm = pl.BlockSpec(memory_space=pl.ANY)
    return pl.pallas_call(
        down_kernel,
        grid=(1,),
        out_shape=jax.ShapeDtypeStruct((128, width), jnp.float32),
        in_specs=[vmem, hbm, hbm],
        out_specs=vmem,
        scratch_shapes=[
            pltpu.VMEM((2 * units + shared, width), jnp.bfloat16),
            pltpu.SemaphoreType.DMA((1 + 2 * width // OSTEP,)),
        ],
        compiler_params=pltpu.CompilerParams(vmem_limit_bytes=16 * 1024 * 1024),
        cost_estimate=pl.CostEstimate(
            flops=2 * 128 * width * (2 * units + shared),
            bytes_accessed=2 * width * (2 * units + shared) + 4 * 128 * width,
            transcendentals=0,
        ),
        name="down",
    )(hid, *[pltpu.with_memory_space_constraint(a, pltpu.HBM) for a in (down, shared_down)])


def prepare_kernel(hidden, routes, slots, weight, out):
    width = hidden.shape[2]
    out[:, :width] = jnp.concatenate([hidden[0], hidden[1]], axis=0).astype(jnp.bfloat16)
    experts = jnp.concatenate([routes[0], routes[1]], axis=0)
    kept = jnp.concatenate([slots[0], slots[1]], axis=0) >= 0
    weights = jnp.where(kept, weight[...].astype(jnp.float32), 0.0)
    lane = lax.broadcasted_iota(jnp.int32, (2, META), 1)
    dense = jnp.zeros((2, META), jnp.float32)
    for k in range(experts.shape[1]):
        dense += jnp.where(lane == experts[:, k : k + 1], weights[:, k : k + 1], 0.0)
    out[:, width:] = dense.astype(jnp.bfloat16)


def prepare(hidden, routes, slots, route_weight):
    steps, _, width = hidden.shape
    return pl.pallas_call(
        prepare_kernel,
        out_shape=pltpu.VMEM((steps, width + META), jnp.bfloat16),
        name="prepare",
    )(hidden, routes, slots, route_weight[:, 0])


def body(
    hidden,
    routes,
    slots,
    route_weight,
    expert_gate,
    expert_up,
    expert_down,
    shared_gate,
    shared_up,
    shared_down,
):
    block = prepare(hidden, routes, slots, route_weight)
    for stage in range(2):
        block = jnp.concatenate([block] + [fetch(block, stage, by) for by in (1, 3, 2)], axis=0)
    mine = [block] + [fetch(block, 2, by) for by in (1, 3, 2)]
    pieces = mine + [swap(piece) for piece in mine]

    first = (2 * lax.axis_index("group")).astype(jnp.int32).reshape(1, 1)
    kept, other = layer(
        pieces, first, expert_gate, expert_up, expert_down, shared_gate, shared_up, shared_down
    )
    other = swap(other)
    total = down_own(kept, expert_down, shared_down) + other.astype(jnp.float32)
    for stage, kind in ((2, jnp.bfloat16), (1, jnp.bfloat16), (0, jnp.float32)):
        count = total.shape[0] // 4
        parts = [total[i * count : (i + 1) * count] for i in range(4)]
        got = [send(part.astype(kind), stage, by) for part, by in zip(parts[:0:-1], (2, 3, 1))]
        total = parts[0]
        for part in got:
            total = total + part.astype(jnp.float32)
    return total[:, None, :]


def solution(mesh):
    return jax.shard_map(
        body,
        mesh=mesh,
        in_specs=(
            P(None, ("group", "local"), None),
            P(None, ("group", "local"), None),
            P(None, ("group", "local"), None),
            P(None, ("group", "local"), None),
            P("group", None, "local"),
            P("group", None, "local"),
            P("group", "local", None),
            P(None, ("group", "local")),
            P(None, ("group", "local")),
            P(("group", "local"), None),
        ),
        out_specs=P(None, ("group", "local"), None),
        check_vma=False,
    )
```
